256 devices in a mesh: tm: 64 (over z, y, x_lo), space: 4 (over x_hi, core).
Axes of the slice: x: 4 (x_hi: 2, x_lo: 2; x = x_hi * 2 + x_lo), y: 4, z: 8, core: 2. Of those that a mesh axis runs over, the one named last changes fastest.
Arguments:
- omega_hat: float32 [512, 256, 256], P('tm', 'space'), may hold values from -1 to 1, as said below
- delta_hat: float32 [512, 256, 256], P('tm', 'space'), may hold values from -1 to 1, as said below
Outputs:
- residual: float32 [512, 256, 256], P('tm', 'space')
- jvp: float32 [512, 256, 256], P('tm', 'space')
The draws below stay inside these ranges and needn't reach their ends.
Inputs may be any that keep to these rules, and one draw needn't show every extreme that they name: `omega_hat`: coefficients of independent draws whose size falls with the wavenumbers. `delta_hat`: coefficients of independent draws whose size falls with the wavenumbers.
All inputs are finite; a program needn't handle non-finite values.
Results may differ from the reference program's by a relative error of at most 0.0003.
Values sent between devices are 32-bit elements; how exact they have to be, the bound alone decides.
A program may use at most 192 MiB of HBM per device.

```python
import math
import jax
import jax.numpy as jnp
from jax import lax

NT = 512
NX = 256
NY = 256


def wavenumbers(n):
    indices = jnp.arange(n, dtype=jnp.int32)
    return jnp.where(indices == 1, n // 2, indices // 2).astype(jnp.float32)


def envelope(radius, temporal):
    wave_t = wavenumbers(NT)
    wave_x = wavenumbers(NX)
    wave_y = wavenumbers(NY)
    spatial = 1.0 / (1.0 + (wave_x[:, None] ** 2 + wave_y[None, :] ** 2) / (radius * radius))
    timely = 1.0 / (1.0 + wave_t * wave_t / (temporal * temporal))
    return timely[:, None, None] * spatial[None, :, :]


def draw_omega_hat(key, part):
    key = jax.random.fold_in(key, 11)
    shape = (NT, NX, NY)
    noise = jnp.clip(jax.random.normal(key, shape, jnp.float32), -4.0, 4.0)
    return (0.2 * noise * envelope(NX / 16.0, NT / 8.0)).astype(jnp.float32)


def draw_delta_hat(key, part):
    key = jax.random.fold_in(key, 23)
    shape = (NT, NX, NY)
    noise = jnp.clip(jax.random.normal(key, shape, jnp.float32), -4.0, 4.0)
    return (0.2 * noise * envelope(NX / 12.0, NT / 6.0)).astype(jnp.float32)


def setup_inputs(seed: int = 0) -> dict:
    key_list = jax.random.split(jax.random.key(seed), 3)
    return {
        "omega_hat": draw_omega_hat(jax.random.fold_in(key_list[2], 71), 0),
        "delta_hat": draw_delta_hat(jax.random.fold_in(key_list[2], 71), 0),
    }


viscosity = 0.025
frequency = 0.3
forcing_wave = 4


def modes(n, offset, length):
    indices = offset + jnp.arange(length, dtype=jnp.int32)
    wavenum = jnp.where(indices == 1, n // 2, indices // 2).astype(jnp.int32)
    return indices, wavenum


def basis_matrix(n):
    points = jnp.arange(n, dtype=jnp.int32)
    indices, wavenum = modes(n, 0, n)
    angles = ((points[:, None] * wavenum[None, :]) % n).astype(jnp.float32) * (2.0 * math.pi / n)
    is_sine = (indices % 2 == 1) & (indices != 1)
    return jnp.where(is_sine[None, :], jnp.sin(angles), jnp.cos(angles))


def forward_matrix(n):
    indices, wavenum = modes(n, 0, n)
    weights = jnp.where(indices < 2, 1.0 / n, 2.0 / n).astype(jnp.float32)
    return basis_matrix(n).T * weights[:, None]


def derivative(values, axis_pos, offset, n):
    shape = values.shape
    length = shape[axis_pos]
    indices, wavenum = modes(n, offset, length)
    factor = jnp.where(indices >= 2, jnp.where(indices % 2 == 0, wavenum, -wavenum), 0).astype(jnp.float32)
    factor = factor.reshape((length,) + (1,) * (len(shape) - axis_pos - 1))
    paired = shape[:axis_pos] + (length // 2, 2) + shape[axis_pos + 1:]
    swapped = jnp.flip(values.reshape(paired), axis_pos + 1).reshape(shape)
    return swapped * factor


def spectral_fields(omega, delta, kx_offset, n_x, n_y):
    indices_x, wave_x = modes(n_x, kx_offset, omega.shape[1])
    indices_y, wave_y = modes(n_y, 0, omega.shape[2])
    wave_x = wave_x.astype(jnp.float32)
    wave_y = wave_y.astype(jnp.float32)
    wave_sq = wave_x[:, None] * wave_x[:, None] + wave_y[None, :] * wave_y[None, :]
    inverse = jnp.where(wave_sq > 0, 1.0 / jnp.maximum(wave_sq, 1.0), 0.0)
    stream = omega * inverse
    stream_delta = delta * inverse
    stacked = jnp.stack([
        derivative(stream, 2, 0, n_y),
        -derivative(stream, 1, kx_offset, n_x),
        derivative(omega, 1, kx_offset, n_x),
        derivative(omega, 2, 0, n_y),
        derivative(stream_delta, 2, 0, n_y),
        -derivative(stream_delta, 1, kx_offset, n_x),
        derivative(delta, 1, kx_offset, n_x),
        derivative(delta, 2, 0, n_y),
    ])
    return stacked, wave_sq


def advect(physical):
    velocity_u, velocity_v, omega_dx, omega_dy = physical[0], physical[1], physical[2], physical[3]
    delta_u, delta_v, delta_dx, delta_dy = physical[4], physical[5], physical[6], physical[7]
    advection = velocity_u * omega_dx + velocity_v * omega_dy
    linearized = velocity_u * delta_dx + velocity_v * delta_dy + delta_u * omega_dx + delta_v * omega_dy
    return jnp.stack([advection, linearized])


def assemble(omega, delta, nonlinear, wave_sq, kt_offset, kx_offset, n_t):
    idx_t = kt_offset + jnp.arange(omega.shape[0], dtype=jnp.int32)
    idx_x = kx_offset + jnp.arange(omega.shape[1], dtype=jnp.int32)
    idx_y = jnp.arange(omega.shape[2], dtype=jnp.int32)
    marked = (idx_t == 0)[:, None, None] & (idx_x == 0)[None, :, None] & (idx_y == 2 * forcing_wave)[None, None, :]
    forcing = jnp.where(marked, -float(forcing_wave), 0.0).astype(jnp.float32)
    residual = frequency * derivative(omega, 0, kt_offset, n_t) + nonlinear[0] + viscosity * wave_sq * omega - forcing
    tangent = frequency * derivative(delta, 0, kt_offset, n_t) + nonlinear[1] + viscosity * wave_sq * delta
    return residual, tangent


def reference(omega_hat, delta_hat):
    fields, wave_sq = spectral_fields(omega_hat, delta_hat, 0, NX, NY)
    highest = lax.Precision.HIGHEST
    along_y = jnp.einsum('ftxk,yk->ftxy', fields, basis_matrix(NY), precision=highest)
    along_x = jnp.einsum('ftky,xk->ftxy', along_y, basis_matrix(NX), precision=highest)
    physical = jnp.einsum('fkxy,tk->ftxy', along_x, basis_matrix(NT), precision=highest)
    products = advect(physical)
    spectra_t = jnp.einsum('ftxy,kt->fkxy', products, forward_matrix(NT), precision=highest)
    spectra_x = jnp.einsum('ftxy,kx->ftky', spectra_t, forward_matrix(NX), precision=highest)
    nonlinear = jnp.einsum('ftxy,ky->ftxk', spectra_x, forward_matrix(NY), precision=highest)
    return assemble(omega_hat, delta_hat, nonlinear, wave_sq, 0, 0, NT)
```

```python
import functools

import jax
import jax.numpy as jnp
import ml_dtypes
import numpy as np
from jax import lax
from jax.experimental import pallas as pl
from jax.experimental.pallas import tpu as pltpu
from jax.sharding import PartitionSpec as P

MESH = pl.DeviceIdType.MESH
viscosity = 0.025
frequency = 0.3
forcing_wave = 4

NT, NX, NY = 512, 256, 256
GROUP = 2
OUTER = 256 // GROUP
ROWS = 4 * GROUP
SPAN = NT // GROUP


def wavenumbers(n):
    indices = np.arange(n)
    return np.where(indices == 1, n // 2, indices // 2)


def basis_matrix(n):
    points, indices, wave = np.arange(n), np.arange(n), wavenumbers(n)
    angles = (points[:, None] * wave[None, :] % n) * (2.0 * np.pi / n)
    is_sine = (indices % 2 == 1) & (indices != 1)
    return np.where(is_sine[None, :], np.sin(angles), np.cos(angles))


def forward_matrix(n):
    weights = np.where(np.arange(n) < 2, 1.0 / n, 2.0 / n)
    return basis_matrix(n).T * weights[:, None]


def derivative_matrix(n):
    wave = wavenumbers(n)
    out = np.zeros((n, n))
    for j in range(2, n):
        if j % 2 == 0:
            out[j, j + 1] = wave[j]
        else:
            out[j, j - 1] = -wave[j]
    return out


def split_constant(matrix):
    high = matrix.astype(np.float32).astype(ml_dtypes.bfloat16)
    low = (matrix - high.astype(np.float64)).astype(np.float32).astype(ml_dtypes.bfloat16)
    return [high, low]


def x_order():
    core, x_hi, tm = np.meshgrid(np.arange(2), np.arange(2), np.arange(64), indexing="ij")
    return (128 * x_hi + 64 * core + tm).reshape(-1)


def constants():
    order = x_order()
    synth_t, forward_t = basis_matrix(NT), forward_matrix(NT)
    synth_x, synth_y = basis_matrix(NX), basis_matrix(NY)
    slope_x = (synth_x @ derivative_matrix(NX))[:, order]
    slope_y = synth_y @ derivative_matrix(NY)
    time = np.stack(split_constant(synth_t) + split_constant(forward_t))
    space = np.stack(
        split_constant(synth_x[:, order])
        + split_constant(slope_x)
        + split_constant(synth_y.T)
        + split_constant(slope_y.T)
        + split_constant(forward_matrix(NX)[order])
        + split_constant(forward_matrix(NY).T)
    )
    wave_x, wave_y = wavenumbers(NX)[order], wavenumbers(NY)
    square = (wave_x[:, None] ** 2 + wave_y[None, :] ** 2).astype(np.float64)
    inverse = np.where(square > 0, 1.0 / np.maximum(square, 1.0), 0.0).astype(np.float32)
    return time, space, inverse


def halves(value):
    high = value.astype(jnp.bfloat16)
    return high, (value - high.astype(jnp.float32)).astype(jnp.bfloat16)


def product(left, right):
    dot = functools.partial(jnp.dot, preferred_element_type=jnp.float32)
    return dot(left[0], right[0]) + (dot(left[1], right[0]) + dot(left[0], right[1]))


def both(ref, *index):
    return jnp.concatenate([ref[(*index, h)] for h in range(2)], axis=1)


def kernel(
    omega_ref,
    delta_ref,
    time_hbm,
    space_hbm,
    inverse_hbm,
    residual_ref,
    jvp_ref,
    time_ref,
    space_ref,
    inverse_ref,
    a_src,
    a_dst,
    c1_src,
    c1_dst,
    c2_src,
    c2_dst,
    fields,
    r2_src,
    r2_dst,
    r1_src,
    r1_dst,
    b_src,
    b_dst,
    linear,
    const_sem,
    send_sem,
    recv_sem,
):
    tm, space = lax.axis_index("tm"), lax.axis_index("space")
    z, y, x_lo, x_hi, core = tm // 8, (tm // 2) % 4, tm % 2, space // 2, space % 2
    outer = x_hi * 64 + tm
    inputs = (omega_ref, delta_ref)

    loads = [
        pltpu.make_async_copy(src, dst, const_sem.at[k])
        for k, (src, dst) in enumerate(
            ((time_hbm, time_ref), (space_hbm, space_ref), (inverse_hbm, inverse_ref))
        )
    ]
    for load in loads:
        load.start()

    def tm_partner(step):
        dz, dy, dx = (3 * step) % 8, (step // 8) % 4, step // 32
        return ((z + dz) % 8) * 8 + ((y + dy) % 4) * 2 + (x_lo + dx) % 2

    def outer_partner(step):
        dz, dy, dx = (3 * step) % 8, (step // 8) % 4, step // 32
        x = (x_hi * 2 + x_lo + dx) % 4
        return ((z + dz) % 8) * 8 + ((y + dy) % 4) * 2 + x % 2, x // 2

    def settle(buffer, sem):
        pltpu.make_async_copy(buffer, buffer, sem).wait()

    def rows8(index):
        return pl.ds(pl.multiple_of(index * 8, 8), 8)

    def exchange_tm(stage, a, src, dst):
        send, recv = send_sem.at[stage, a], recv_sem.at[stage, a]
        pltpu.make_async_copy(src.at[a, :, rows8(tm)], dst.at[a, :, rows8(tm)], recv).start()

        def body(step, carry):
            partner = tm_partner(step)
            pltpu.make_async_remote_copy(
                src_ref=src.at[a, :, rows8(partner)],
                dst_ref=dst.at[a, :, rows8(tm)],
                send_sem=send,
                recv_sem=recv,
                device_id=(partner, space),
                device_id_type=MESH,
            ).start()
            return carry

        lax.fori_loop(1, 64, body, 0)

    def message(index):
        return pl.ds(pl.multiple_of(index * ROWS, ROWS), ROWS)

    def exchange_outer(stage, a, src, dst):
        send, recv = send_sem.at[stage, a], recv_sem.at[stage, a]
        pltpu.make_async_copy(src.at[a, message(outer)], dst.at[a, message(outer)], recv).start()

        def body(step, carry):
            partner, partner_hi = outer_partner(step)
            pltpu.make_async_remote_copy(
                src_ref=src.at[a, message(partner_hi * 64 + partner)],
                dst_ref=dst.at[a, message(outer)],
                send_sem=send,
                recv_sem=recv,
                device_id=(partner, partner_hi * 2 + core),
                device_id_type=MESH,
            ).start()
            return carry

        lax.fori_loop(1, OUTER, body, 0)

    def span(index):
        return pl.ds(pl.multiple_of(index * SPAN, SPAN), SPAN)

    sibling = (tm, x_hi * 2 + (1 - core))

    def gather_group(a):
        send, recv = send_sem.at[1, a], recv_sem.at[1, a]
        pltpu.make_async_copy(c1_src.at[a, :, span(core)], c1_dst.at[a, core], recv).start()
        pltpu.make_async_remote_copy(
            src_ref=c1_src.at[a, :, span(1 - core)],
            dst_ref=c1_dst.at[a, core],
            send_sem=send,
            recv_sem=recv,
            device_id=sibling,
            device_id_type=MESH,
        ).start()

    def scatter_group(a):
        send, recv = send_sem.at[4, a], recv_sem.at[4, a]
        pltpu.make_async_copy(r1_src.at[a, core], r1_dst.at[a, :, span(core)], recv).start()
        pltpu.make_async_remote_copy(
            src_ref=r1_src.at[a, 1 - core],
            dst_ref=r1_dst.at[a, :, span(core)],
            send_sem=send,
            recv_sem=recv,
            device_id=sibling,
            device_id_type=MESH,
        ).start()

    def time_transform(which, value):
        matrix = (time_ref[which], time_ref[which + 1])
        return product(matrix, halves(value))

    def lane_row(half, point, member):
        return pl.ds((half * 2 + point) * GROUP + member, OUTER, stride=ROWS)

    for a in range(2):
        for r in range(8):
            for h in range(2):
                a_src[a, h, pl.ds(r, 64, stride=8), :] = inputs[a][r, :, h * 128 : h * 128 + 128]
        exchange_tm(0, a, a_src, a_dst)

    row = lax.broadcasted_iota(jnp.int32, (64, NY), 0) + space * 64
    col = lax.broadcasted_iota(jnp.int32, (64, NY), 1)
    wave_x = jnp.where(row == 1, NX // 2, row // 2).astype(jnp.float32)
    wave_y = jnp.where(col == 1, NY // 2, col // 2).astype(jnp.float32)
    damping = viscosity * (wave_x * wave_x + wave_y * wave_y)
    forced = (row == 0) & (col == 2 * forcing_wave)
    for a in range(2):
        for r in range(8):
            wave_t = (tm * 4 + r // 2).astype(jnp.float32)
            rate = frequency * wave_t if r % 2 == 0 else -frequency * wave_t
            term = rate * inputs[a][r ^ 1] + damping * inputs[a][r]
            if a == 0 and r == 0:
                force = jnp.where(tm == 0, -float(forcing_wave), 0.0).astype(jnp.float32)
                term = term - jnp.where(forced, force, 0.0)
            linear[a, r] = term

    for load in loads:
        load.wait()

    for a in range(2):
        settle(a_dst.at[a], recv_sem.at[0, a])
        value = time_transform(0, both(a_dst, a))
        for h in range(2):
            c1_src[a, h] = value[:, h * 128 : h * 128 + 128]
        gather_group(a)
        settle(c1_dst.at[a], recv_sem.at[1, a])
        for g in range(GROUP):
            for h in range(2):
                for t in range(2):
                    c2_src[a, lane_row(h, t, g), :] = c1_dst[a, g, h, t * OUTER : (t + 1) * OUTER, :]
        exchange_outer(2, a, c2_src, c2_dst)

    for a in range(2):
        settle(c2_dst.at[a], recv_sem.at[2, a])
        planes = []
        for t in range(2):
            columns = [
                jnp.concatenate([c2_dst[a, lane_row(h, t, g), :] for g in range(GROUP)], axis=0)
                for h in range(2)
            ]
            planes.append(jnp.concatenate(columns, axis=1))
        inverse = inverse_ref[...]
        right = halves(jnp.concatenate([inverse * planes[0], inverse * planes[1]] + planes, axis=1))
        for k, (along_x, along_y) in enumerate(((0, 6), (2, 4))):
            mixed = product((space_ref[along_x], space_ref[along_x + 1]), right)
            stacked = jnp.concatenate([mixed[:, q * 256 : q * 256 + 256] for q in range(4)], axis=0)
            grid = product(halves(stacked), (space_ref[along_y], space_ref[along_y + 1]))
            for q in range(4):
                fields[a, k, q] = grid[q * 256 : q * 256 + 256]
        points = []
        for t in range(2):
            total = fields[0, 0, t] * fields[a, 1, 2 + t] - fields[0, 1, t] * fields[a, 0, 2 + t]
            if a == 1:
                total = total + (
                    fields[1, 0, t] * fields[0, 1, 2 + t] - fields[1, 1, t] * fields[0, 0, 2 + t]
                )
            points.append(total)
        mixed = product((space_ref[8], space_ref[9]), halves(jnp.concatenate(points, axis=1)))
        stacked = jnp.concatenate([mixed[:, :256], mixed[:, 256:]], axis=0)
        modes = product(halves(stacked), (space_ref[10], space_ref[11]))
        for t in range(2):
            for g in range(GROUP):
                for h in range(2):
                    start = t * 256 + g * OUTER
                    r2_src[a, lane_row(h, t, g), :] = modes[
                        start : start + OUTER, h * 128 : h * 128 + 128
                    ]
        exchange_outer(3, a, r2_src, r2_dst)

    for a in range(2):
        settle(r2_dst.at[a], recv_sem.at[3, a])
        for g in range(GROUP):
            for h in range(2):
                for t in range(2):
                    r1_src[a, g, h, t * OUTER : (t + 1) * OUTER, :] = r2_dst[a, lane_row(h, t, g), :]
        scatter_group(a)
        settle(r1_dst.at[a], recv_sem.at[4, a])
        value = time_transform(2, both(r1_dst, a))
        for h in range(2):
            b_src[a, h] = value[:, h * 128 : h * 128 + 128]
        exchange_tm(5, a, b_src, b_dst)

    outputs = (residual_ref, jvp_ref)
    for a in range(2):
        settle(b_dst.at[a], recv_sem.at[5, a])
        for r in range(8):
            for h in range(2):
                lanes = slice(h * 128, h * 128 + 128)
                outputs[a][r, :, lanes] = linear[a, r, :, lanes] + b_dst[a, h, pl.ds(r, 64, stride=8), :]

    for a in range(2):
        settle(a_src.at[a, :, pl.ds(0, NT - 8)], send_sem.at[0, a])
        settle(c1_src.at[a, :, pl.ds(0, SPAN)], send_sem.at[1, a])
        settle(c2_src.at[a, pl.ds(0, 1024 - ROWS)], send_sem.at[2, a])
        settle(r2_src.at[a, pl.ds(0, 1024 - ROWS)], send_sem.at[3, a])
        settle(r1_src.at[a, 0], send_sem.at[4, a])
        settle(b_src.at[a, :, pl.ds(0, NT - 8)], send_sem.at[5, a])


def solution(mesh):
    time, space, inverse = constants()

    def per_device(omega, delta):
        block = jax.ShapeDtypeStruct(omega.shape, jnp.float32)
        vmem, anywhere = pl.BlockSpec(memory_space=pltpu.VMEM), pl.BlockSpec(memory_space=pl.ANY)
        strips = pltpu.VMEM((2, 2, NT, 128), jnp.float32)
        pieces = pltpu.VMEM((2, GROUP, 2, SPAN, 128), jnp.float32)
        tiles = pltpu.VMEM((2, OUTER * ROWS, 128), jnp.float32)
        return pl.pallas_call(
            kernel,
            out_shape=(block, block),
            in_specs=[vmem, vmem, anywhere, anywhere, anywhere],
            out_specs=(vmem, vmem),
            scratch_shapes=[
                pltpu.VMEM(time.shape, jnp.bfloat16),
                pltpu.VMEM(space.shape, jnp.bfloat16),
                pltpu.VMEM(inverse.shape, jnp.float32),
                strips,
                strips,
                strips,
                pieces,
                tiles,
                tiles,
                pltpu.VMEM((2, 2, 4, NX, NY), jnp.float32),
                tiles,
                tiles,
                pieces,
                strips,
                strips,
                strips,
                pltpu.VMEM((2, 8, 64, NY), jnp.float32),
                pltpu.SemaphoreType.DMA((3,)),
                pltpu.SemaphoreType.DMA((6, 2)),
                pltpu.SemaphoreType.DMA((6, 2)),
            ],
            compiler_params=pltpu.CompilerParams(
                has_side_effects=True, vmem_limit_bytes=58 * 1024 * 1024
            ),
        )(omega, delta, time, space, inverse)

    specs = (P("tm", "space", None), P("tm", "space", None))
    return jax.shard_map(per_device, mesh=mesh, in_specs=specs, out_specs=specs, check_vma=False)
```

```python
import functools

import jax
import jax.numpy as jnp
import ml_dtypes
import numpy as np
from jax import lax
from jax.experimental import pallas as pl
from jax.experimental.pallas import tpu as pltpu
from jax.sharding import PartitionSpec as P

MESH = pl.DeviceIdType.MESH
viscosity = 0.025
frequency = 0.3
forcing_wave = 4

NT, NX, NY = 512, 256, 256
GROUP = 2
OUTER = 256 // GROUP
ROWS = 4 * GROUP
SPAN = NT // GROUP


def wavenumbers(n):
    indices = np.arange(n)
    return np.where(indices == 1, n // 2, indices // 2)


def basis_matrix(n):
    points, indices, wave = np.arange(n), np.arange(n), wavenumbers(n)
    angles = (points[:, None] * wave[None, :] % n) * (2.0 * np.pi / n)
    is_sine = (indices % 2 == 1) & (indices != 1)
    return np.where(is_sine[None, :], np.sin(angles), np.cos(angles))


def forward_matrix(n):
    weights = np.where(np.arange(n) < 2, 1.0 / n, 2.0 / n)
    return basis_matrix(n).T * weights[:, None]


def derivative_matrix(n):
    wave = wavenumbers(n)
    out = np.zeros((n, n))
    for j in range(2, n):
        if j % 2 == 0:
            out[j, j + 1] = wave[j]
        else:
            out[j, j - 1] = -wave[j]
    return out


def split_constant(matrix):
    high = matrix.astype(np.float32).astype(ml_dtypes.bfloat16)
    low = (matrix - high.astype(np.float64)).astype(np.float32).astype(ml_dtypes.bfloat16)
    return [high, low]


def x_order():
    core, x_hi, tm = np.meshgrid(np.arange(2), np.arange(2), np.arange(64), indexing="ij")
    return (128 * x_hi + 64 * core + tm).reshape(-1)


def constants():
    order = x_order()
    synth_t, forward_t = basis_matrix(NT), forward_matrix(NT)
    synth_x, synth_y = basis_matrix(NX), basis_matrix(NY)
    slope_x = (synth_x @ derivative_matrix(NX))[:, order]
    slope_y = synth_y @ derivative_matrix(NY)
    time = np.stack(split_constant(synth_t) + split_constant(forward_t))
    space = np.stack(
        split_constant(synth_x[:, order])
        + split_constant(slope_x)
        + split_constant(synth_y.T)
        + split_constant(slope_y.T)
        + split_constant(forward_matrix(NX)[order])
        + split_constant(forward_matrix(NY).T)
    )
    wave_x, wave_y = wavenumbers(NX)[order], wavenumbers(NY)
    square = (wave_x[:, None] ** 2 + wave_y[None, :] ** 2).astype(np.float64)
    inverse = np.where(square > 0, 1.0 / np.maximum(square, 1.0), 0.0).astype(np.float32)
    return time, space, inverse


def halves(value):
    high = value.astype(jnp.bfloat16)
    return high, (value - high.astype(jnp.float32)).astype(jnp.bfloat16)


def product(left, right):
    dot = functools.partial(jnp.dot, preferred_element_type=jnp.float32)
    return dot(left[0], right[0]) + (dot(left[1], right[0]) + dot(left[0], right[1]))


def both(ref, *index):
    return jnp.concatenate([ref[(*index, h)] for h in range(2)], axis=1)


def kernel(
    omega_hbm,
    delta_hbm,
    time_hbm,
    space_hbm,
    inverse_hbm,
    residual_ref,
    jvp_ref,
    omega_ref,
    delta_ref,
    time_ref,
    space_ref,
    inverse_ref,
    a_src,
    a_dst,
    c1_src,
    c1_dst,
    c2_src,
    c2_dst,
    fields,
    r2_src,
    r2_dst,
    r1_src,
    r1_dst,
    b_src,
    b_dst,
    linear,
    const_sem,
    send_sem,
    recv_sem,
    plane_sem,
):
    tm, space = lax.axis_index("tm"), lax.axis_index("space")
    z, y, x_lo, x_hi, core = tm // 8, (tm // 2) % 4, tm % 2, space // 2, space % 2
    outer = x_hi * 64 + tm
    inputs = (omega_ref, delta_ref)

    loads = [
        pltpu.make_async_copy(src, dst, const_sem.at[k])
        for k, (src, dst) in enumerate(
            (
                (omega_hbm, omega_ref),
                (delta_hbm, delta_ref),
                (time_hbm, time_ref),
                (space_hbm, space_ref),
                (inverse_hbm, inverse_ref),
            )
        )
    ]

    barrier = pltpu.get_barrier_semaphore()
    column = [(((z + dz) % 8) * 8 + y * 2 + x_lo, space) for dz in range(1, 8)]
    greeted = column + [(tm, x_hi * 2 + (1 - core))]
    for dy in range(4):
        for dx in range(4):
            if dy or dx:
                x = (x_hi * 2 + x_lo + dx) % 4
                greeted.append((z * 8 + ((y + dy) % 4) * 2 + x % 2, (x // 2) * 2 + core))
    for device in greeted:
        pl.semaphore_signal(barrier, inc=1, device_id=device, device_id_type=MESH)
    for load in loads:
        load.start()

    def far_first(step, plane):
        later = step - plane
        level = later // (2 * plane)
        distance = jnp.where(step < plane, 4, (3 - level) * (1 - 2 * (later % 2)))
        place = jnp.where(step < plane, step, (later % (2 * plane)) // 2)
        return distance, jnp.where(level < 3, place, later - 6 * plane + 1)

    def tm_partner(step):
        dz, place = far_first(step, 8)
        return ((z + dz + 8) % 8) * 8 + ((y + place // 2) % 4) * 2 + (x_lo + place) % 2

    def outer_partner(step):
        dz, place = far_first(step, 16)
        x = (x_hi * 2 + x_lo + place) % 4
        return ((z + dz + 8) % 8) * 8 + ((y + place // 4) % 4) * 2 + x % 2, x // 2

    def settle(buffer, sem):
        pltpu.make_async_copy(buffer, buffer, sem).wait()

    def rows8(index):
        return pl.ds(pl.multiple_of(index * 8, 8), 8)

    def exchange_tm(stage, a, src, dst):
        send, recv = send_sem.at[stage, a], recv_sem.at[stage, a]
        pltpu.make_async_copy(src.at[a, :, rows8(tm)], dst.at[a, :, rows8(tm)], recv).start()

        def body(step, carry):
            partner = tm_partner(step)
            pltpu.make_async_remote_copy(
                src_ref=src.at[a, :, rows8(partner)],
                dst_ref=dst.at[a, :, rows8(tm)],
                send_sem=send,
                recv_sem=recv,
                device_id=(partner, space),
                device_id_type=MESH,
            ).start()
            return carry

        lax.fori_loop(0, 63, body, 0)

    def message(index):
        return pl.ds(pl.multiple_of(index * ROWS, ROWS), ROWS)

    def exchange_outer(stage, a, src, dst):
        send, recv = send_sem.at[stage, a], recv_sem.at[stage, a]
        pltpu.make_async_copy(src.at[a, message(outer)], dst.at[a, message(outer)], recv).start()

        def body(step, carry):
            partner, partner_hi = outer_partner(step)
            pltpu.make_async_remote_copy(
                src_ref=src.at[a, message(partner_hi * 64 + partner)],
                dst_ref=dst.at[a, message(outer)],
                send_sem=send,
                recv_sem=recv,
                device_id=(partner, partner_hi * 2 + core),
                device_id_type=MESH,
            ).start()
            return carry

        lax.fori_loop(0, OUTER - 1, body, 0)

    def span(index):
        return pl.ds(pl.multiple_of(index * SPAN, SPAN), SPAN)

    sibling = (tm, x_hi * 2 + (1 - core))

    def gather_group(a):
        send, recv = send_sem.at[1, a], recv_sem.at[1, a]
        pltpu.make_async_copy(c1_src.at[a, :, span(core)], c1_dst.at[a, core], recv).start()
        pltpu.make_async_remote_copy(
            src_ref=c1_src.at[a, :, span(1 - core)],
            dst_ref=c1_dst.at[a, core],
            send_sem=send,
            recv_sem=recv,
            device_id=sibling,
            device_id_type=MESH,
        ).start()

    def scatter_group(a):
        send, recv = send_sem.at[4, a], recv_sem.at[4, a]
        pltpu.make_async_copy(r1_src.at[a, core], r1_dst.at[a, :, span(core)], recv).start()
        pltpu.make_async_remote_copy(
            src_ref=r1_src.at[a, 1 - core],
            dst_ref=r1_dst.at[a, :, span(core)],
            send_sem=send,
            recv_sem=recv,
            device_id=sibling,
            device_id_type=MESH,
        ).start()

    def time_transform(which, value):
        matrix = (time_ref[which], time_ref[which + 1])
        return product(matrix, halves(value))

    def lane_row(half, point, member):
        return pl.ds((half * 2 + point) * GROUP + member, OUTER, stride=ROWS)

    for a in range(2):
        loads[a].wait()
        for r in range(8):
            for h in range(2):
                a_src[a, h, pl.ds(r, 64, stride=8), :] = inputs[a][r, :, h * 128 : h * 128 + 128]
    pl.semaphore_wait(barrier, len(greeted))
    for device in column:
        pl.semaphore_signal(plane_sem, inc=1, device_id=device, device_id_type=MESH)
    pl.semaphore_wait(plane_sem, len(column))
    for a in range(2):
        exchange_tm(0, a, a_src, a_dst)

    row = lax.broadcasted_iota(jnp.int32, (64, NY), 0) + space * 64
    col = lax.broadcasted_iota(jnp.int32, (64, NY), 1)
    wave_x = jnp.where(row == 1, NX // 2, row // 2).astype(jnp.float32)
    wave_y = jnp.where(col == 1, NY // 2, col // 2).astype(jnp.float32)
    damping = viscosity * (wave_x * wave_x + wave_y * wave_y)
    forced = (row == 0) & (col == 2 * forcing_wave)
    for a in range(2):
        for r in range(8):
            wave_t = (tm * 4 + r // 2).astype(jnp.float32)
            rate = frequency * wave_t if r % 2 == 0 else -frequency * wave_t
            term = rate * inputs[a][r ^ 1] + damping * inputs[a][r]
            if a == 0 and r == 0:
                force = jnp.where(tm == 0, -float(forcing_wave), 0.0).astype(jnp.float32)
                term = term - jnp.where(forced, force, 0.0)
            linear[a, r] = term

    for load in loads[2:]:
        load.wait()

    for a in range(2):
        settle(a_dst.at[a], recv_sem.at[0, a])
        value = time_transform(0, both(a_dst, a))
        for h in range(2):
            c1_src[a, h] = value[:, h * 128 : h * 128 + 128]
        gather_group(a)
        settle(c1_dst.at[a], recv_sem.at[1, a])
        for g in range(GROUP):
            for h in range(2):
                for t in range(2):
                    c2_src[a, lane_row(h, t, g), :] = c1_dst[a, g, h, t * OUTER : (t + 1) * OUTER, :]
        exchange_outer(2, a, c2_src, c2_dst)

    for a in range(2):
        settle(c2_dst.at[a], recv_sem.at[2, a])
        planes = []
        for t in range(2):
            columns = [
                jnp.concatenate([c2_dst[a, lane_row(h, t, g), :] for g in range(GROUP)], axis=0)
                for h in range(2)
            ]
            planes.append(jnp.concatenate(columns, axis=1))
        inverse = inverse_ref[...]
        right = halves(jnp.concatenate([inverse * planes[0], inverse * planes[1]] + planes, axis=1))
        for k, (along_x, along_y) in enumerate(((0, 6), (2, 4))):
            mixed = product((space_ref[along_x], space_ref[along_x + 1]), right)
            stacked = jnp.concatenate([mixed[:, q * 256 : q * 256 + 256] for q in range(4)], axis=0)
            grid = product(halves(stacked), (space_ref[along_y], space_ref[along_y + 1]))
            for q in range(4):
                fields[a, k, q] = grid[q * 256 : q * 256 + 256]
        points = []
        for t in range(2):
            total = fields[0, 0, t] * fields[a, 1, 2 + t] - fields[0, 1, t] * fields[a, 0, 2 + t]
            if a == 1:
                total = total + (
                    fields[1, 0, t] * fields[0, 1, 2 + t] - fields[1, 1, t] * fields[0, 0, 2 + t]
                )
            points.append(total)
        mixed = product((space_ref[8], space_ref[9]), halves(jnp.concatenate(points, axis=1)))
        stacked = jnp.concatenate([mixed[:, :256], mixed[:, 256:]], axis=0)
        modes = product(halves(stacked), (space_ref[10], space_ref[11]))
        for t in range(2):
            for g in range(GROUP):
                for h in range(2):
                    start = t * 256 + g * OUTER
                    r2_src[a, lane_row(h, t, g), :] = modes[
                        start : start + OUTER, h * 128 : h * 128 + 128
                    ]
        exchange_outer(3, a, r2_src, r2_dst)

    for a in range(2):
        settle(r2_dst.at[a], recv_sem.at[3, a])
        for g in range(GROUP):
            for h in range(2):
                for t in range(2):
                    r1_src[a, g, h, t * OUTER : (t + 1) * OUTER, :] = r2_dst[a, lane_row(h, t, g), :]
        scatter_group(a)
        settle(r1_dst.at[a], recv_sem.at[4, a])
        value = time_transform(2, both(r1_dst, a))
        for h in range(2):
            b_src[a, h] = value[:, h * 128 : h * 128 + 128]
        exchange_tm(5, a, b_src, b_dst)

    outputs = (residual_ref, jvp_ref)
    for a in range(2):
        settle(b_dst.at[a], recv_sem.at[5, a])
        for r in range(8):
            for h in range(2):
                lanes = slice(h * 128, h * 128 + 128)
                outputs[a][r, :, lanes] = linear[a, r, :, lanes] + b_dst[a, h, pl.ds(r, 64, stride=8), :]

    for a in range(2):
        settle(a_src.at[a, :, pl.ds(0, NT - 8)], send_sem.at[0, a])
        settle(c1_src.at[a, :, pl.ds(0, SPAN)], send_sem.at[1, a])
        settle(c2_src.at[a, pl.ds(0, 1024 - ROWS)], send_sem.at[2, a])
        settle(r2_src.at[a, pl.ds(0, 1024 - ROWS)], send_sem.at[3, a])
        settle(r1_src.at[a, 0], send_sem.at[4, a])
        settle(b_src.at[a, :, pl.ds(0, NT - 8)], send_sem.at[5, a])


PARTS = 2


def hand_over(residual_in, jvp_in, residual_ref, jvp_ref, one, two, sem, out_sem):
    copies, outs = [], []
    for a, (src, mid, dst) in enumerate(((residual_in, one, residual_ref), (jvp_in, two, jvp_ref))):
        for k in range(PARTS):
            part = pl.ds(k * (8 // PARTS), 8 // PARTS)
            copies.append(pltpu.make_async_copy(src.at[part], mid.at[part], sem.at[a, k]))
            outs.append(pltpu.make_async_copy(mid.at[part], dst.at[part], out_sem.at[a, k]))
    for copy in copies:
        copy.start()
    for copy, out in zip(copies, outs):
        copy.wait()
        out.start()
    for out in outs:
        out.wait()


def solution(mesh):
    time, space, inverse = constants()

    def per_device(omega, delta):
        block = jax.ShapeDtypeStruct(omega.shape, jnp.float32)
        vmem, main = pl.BlockSpec(memory_space=pltpu.VMEM), pl.BlockSpec(memory_space=pltpu.HBM)
        strips = pltpu.VMEM((2, 2, NT, 128), jnp.float32)
        pieces = pltpu.VMEM((2, GROUP, 2, SPAN, 128), jnp.float32)
        tiles = pltpu.VMEM((2, OUTER * ROWS, 128), jnp.float32)
        results = pl.pallas_call(
            kernel,
            out_shape=(block, block),
            in_specs=[main] * 5,
            out_specs=(vmem, vmem),
            scratch_shapes=[
                pltpu.VMEM(block.shape, jnp.float32),
                pltpu.VMEM(block.shape, jnp.float32),
                pltpu.VMEM(time.shape, jnp.bfloat16),
                pltpu.VMEM(space.shape, jnp.bfloat16),
                pltpu.VMEM(inverse.shape, jnp.float32),
                strips,
                strips,
                strips,
                pieces,
                tiles,
                tiles,
                pltpu.VMEM((2, 2, 4, NX, NY), jnp.float32),
                tiles,
                tiles,
                pieces,
                strips,
                strips,
                strips,
                pltpu.VMEM((2, 8, 64, NY), jnp.float32),
                pltpu.SemaphoreType.DMA((5,)),
                pltpu.SemaphoreType.DMA((6, 2)),
                pltpu.SemaphoreType.DMA((6, 2)),
                pltpu.SemaphoreType.REGULAR,
            ],
            compiler_params=pltpu.CompilerParams(
                collective_id=0, has_side_effects=True, vmem_limit_bytes=58 * 1024 * 1024
            ),
        )(omega, delta, time, space, inverse)
        return pl.pallas_call(
            hand_over,
            out_shape=(block, block),
            in_specs=[main] * 2,
            out_specs=(main, main),
            scratch_shapes=[pltpu.VMEM(block.shape, jnp.float32), pltpu.VMEM(block.shape, jnp.float32), pltpu.SemaphoreType.DMA((2, PARTS)), pltpu.SemaphoreType.DMA((2, PARTS))],
            compiler_params=pltpu.CompilerParams(vmem_limit_bytes=60 * 1024 * 1024),
        )(*results)

    specs = (P("tm", "space", None), P("tm", "space", None))
    return jax.shard_map(per_device, mesh=mesh, in_specs=specs, out_specs=specs, check_vma=False)
```

```python
import functools

import jax
import jax.numpy as jnp
import ml_dtypes
import numpy as np
from jax import lax
from jax.experimental import pallas as pl
from jax.experimental.pallas import tpu as pltpu
from jax.sharding import PartitionSpec as P

MESH = pl.DeviceIdType.MESH
viscosity = 0.025
frequency = 0.3
forcing_wave = 4

NT, NX, NY = 512, 256, 256
GROUP = 2
OUTER = 256 // GROUP
ROWS = 4 * GROUP
SPAN = NT // GROUP


def wavenumbers(n):
    indices = np.arange(n)
    return np.where(indices == 1, n // 2, indices // 2)


def basis_matrix(n):
    points, indices, wave = np.arange(n), np.arange(n), wavenumbers(n)
    angles = (points[:, None] * wave[None, :] % n) * (2.0 * np.pi / n)
    is_sine = (indices % 2 == 1) & (indices != 1)
    return np.where(is_sine[None, :], np.sin(angles), np.cos(angles))


def forward_matrix(n):
    weights = np.where(np.arange(n) < 2, 1.0 / n, 2.0 / n)
    return basis_matrix(n).T * weights[:, None]


def derivative_matrix(n):
    wave = wavenumbers(n)
    out = np.zeros((n, n))
    for j in range(2, n):
        if j % 2 == 0:
            out[j, j + 1] = wave[j]
        else:
            out[j, j - 1] = -wave[j]
    return out


def split_constant(matrix):
    high = matrix.astype(np.float32).astype(ml_dtypes.bfloat16)
    low = (matrix - high.astype(np.float64)).astype(np.float32).astype(ml_dtypes.bfloat16)
    return [high, low]


def x_order():
    core, x_hi, tm = np.meshgrid(np.arange(2), np.arange(2), np.arange(64), indexing="ij")
    return (128 * x_hi + 64 * core + tm).reshape(-1)


def constants():
    order = x_order()
    synth_t, forward_t = basis_matrix(NT), forward_matrix(NT)
    synth_x, synth_y = basis_matrix(NX), basis_matrix(NY)
    slope_x = (synth_x @ derivative_matrix(NX))[:, order]
    slope_y = synth_y @ derivative_matrix(NY)
    time = np.stack(split_constant(synth_t) + split_constant(forward_t))
    space = np.stack(
        split_constant(synth_x[:, order])
        + split_constant(slope_x)
        + split_constant(synth_y.T)
        + split_constant(slope_y.T)
        + split_constant(forward_matrix(NX)[order])
        + split_constant(forward_matrix(NY).T)
    )
    wave_x, wave_y = wavenumbers(NX)[order], wavenumbers(NY)
    square = (wave_x[:, None] ** 2 + wave_y[None, :] ** 2).astype(np.float64)
    inverse = np.where(square > 0, 1.0 / np.maximum(square, 1.0), 0.0).astype(np.float32)
    return time, space, inverse


def halves(value):
    high = value.astype(jnp.bfloat16)
    return high, (value - high.astype(jnp.float32)).astype(jnp.bfloat16)


def product(left, right):
    dot = functools.partial(jnp.dot, preferred_element_type=jnp.float32)
    return dot(left[0], right[0]) + (dot(left[1], right[0]) + dot(left[0], right[1]))


def both(ref, *index):
    return jnp.concatenate([ref[(*index, h)] for h in range(2)], axis=1)


def kernel(
    omega_hbm,
    delta_hbm,
    time_hbm,
    space_hbm,
    inverse_hbm,
    residual_ref,
    jvp_ref,
    omega_ref,
    delta_ref,
    time_ref,
    space_ref,
    inverse_ref,
    a_src,
    a_dst,
    c1_src,
    c1_dst,
    c2_src,
    c2_dst,
    fields,
    r2_src,
    r2_dst,
    r1_src,
    r1_dst,
    b_src,
    b_dst,
    linear,
    const_sem,
    send_sem,
    recv_sem,
    plane_sem,
):
    tm, space = lax.axis_index("tm"), lax.axis_index("space")
    z, y, x_lo, x_hi, core = tm // 8, (tm // 2) % 4, tm % 2, space // 2, space % 2
    outer = x_hi * 64 + tm
    inputs = (omega_ref, delta_ref)

    loads = [
        pltpu.make_async_copy(src, dst, const_sem.at[k])
        for k, (src, dst) in enumerate(
            (
                (omega_hbm, omega_ref),
                (delta_hbm, delta_ref),
                (time_hbm, time_ref),
                (space_hbm, space_ref),
                (inverse_hbm, inverse_ref),
            )
        )
    ]

    barrier = pltpu.get_barrier_semaphore()
    column = [(((z + dz) % 8) * 8 + y * 2 + x_lo, space) for dz in range(1, 8)]
    greeted = column + [(tm, x_hi * 2 + (1 - core))]
    for dy in range(4):
        for dx in range(4):
            if dy or dx:
                x = (x_hi * 2 + x_lo + dx) % 4
                greeted.append((z * 8 + ((y + dy) % 4) * 2 + x % 2, (x // 2) * 2 + core))
    for device in greeted:
        pl.semaphore_signal(barrier, inc=1, device_id=device, device_id_type=MESH)
    for load in loads:
        load.start()

    def tm_partner(step):
        dz, place = 3 * step, step // 8
        return ((z + dz) % 8) * 8 + ((y + place // 2) % 4) * 2 + (x_lo + place) % 2

    def outer_partner(step):
        dz, place = 3 * step, step // 8
        x = (x_hi * 2 + x_lo + place) % 4
        return ((z + dz) % 8) * 8 + ((y + place // 4) % 4) * 2 + x % 2, x // 2

    def settle(buffer, sem):
        pltpu.make_async_copy(buffer, buffer, sem).wait()

    def rows8(index):
        return pl.ds(pl.multiple_of(index * 8, 8), 8)

    def exchange_tm(stage, a, src, dst, first=0, last=64):
        send, recv = send_sem.at[stage, a], recv_sem.at[stage, a]
        if first == 0:
            pltpu.make_async_copy(src.at[a, :, rows8(tm)], dst.at[a, :, rows8(tm)], recv).start()

        def body(step, carry):
            partner = tm_partner(step)
            pltpu.make_async_remote_copy(
                src_ref=src.at[a, :, rows8(partner)],
                dst_ref=dst.at[a, :, rows8(tm)],
                send_sem=send,
                recv_sem=recv,
                device_id=(partner, space),
                device_id_type=MESH,
            ).start()
            return carry

        lax.fori_loop(max(first, 1), last, body, 0)

    def message(index):
        return pl.ds(pl.multiple_of(index * ROWS, ROWS), ROWS)

    def exchange_outer(stage, a, src, dst):
        send, recv = send_sem.at[stage, a], recv_sem.at[stage, a]
        pltpu.make_async_copy(src.at[a, message(outer)], dst.at[a, message(outer)], recv).start()

        def body(step, carry):
            partner, partner_hi = outer_partner(step)
            pltpu.make_async_remote_copy(
                src_ref=src.at[a, message(partner_hi * 64 + partner)],
                dst_ref=dst.at[a, message(outer)],
                send_sem=send,
                recv_sem=recv,
                device_id=(partner, partner_hi * 2 + core),
                device_id_type=MESH,
            ).start()
            return carry

        lax.fori_loop(1, OUTER, body, 0)

    def span(index):
        return pl.ds(pl.multiple_of(index * SPAN, SPAN), SPAN)

    sibling = (tm, x_hi * 2 + (1 - core))

    def gather_group(a):
        send, recv = send_sem.at[1, a], recv_sem.at[1, a]
        pltpu.make_async_copy(c1_src.at[a, :, span(core)], c1_dst.at[a, core], recv).start()
        pltpu.make_async_remote_copy(
            src_ref=c1_src.at[a, :, span(1 - core)],
            dst_ref=c1_dst.at[a, core],
            send_sem=send,
            recv_sem=recv,
            device_id=sibling,
            device_id_type=MESH,
        ).start()

    def scatter_group(a):
        send, recv = send_sem.at[4, a], recv_sem.at[4, a]
        pltpu.make_async_copy(r1_src.at[a, core], r1_dst.at[a, :, span(core)], recv).start()
        pltpu.make_async_remote_copy(
            src_ref=r1_src.at[a, 1 - core],
            dst_ref=r1_dst.at[a, :, span(core)],
            send_sem=send,
            recv_sem=recv,
            device_id=sibling,
            device_id_type=MESH,
        ).start()

    def time_transform(which, value):
        matrix = (time_ref[which], time_ref[which + 1])
        return product(matrix, halves(value))

    def lane_row(half, point, member):
        return pl.ds((half * 2 + point) * GROUP + member, OUTER, stride=ROWS)

    for a in range(2):
        loads[a].wait()
        for r in range(8):
            for h in range(2):
                a_src[a, h, pl.ds(r, 64, stride=8), :] = inputs[a][r, :, h * 128 : h * 128 + 128]
    pl.semaphore_wait(barrier, len(greeted))
    for device in column:
        pl.semaphore_signal(plane_sem, inc=1, device_id=device, device_id_type=MESH)
    for a in range(2):
        exchange_tm(0, a, a_src, a_dst, 0, 8)
    pl.semaphore_wait(plane_sem, len(column))
    for a in range(2):
        exchange_tm(0, a, a_src, a_dst, 8, 64)

    row = lax.broadcasted_iota(jnp.int32, (64, NY), 0) + space * 64
    col = lax.broadcasted_iota(jnp.int32, (64, NY), 1)
    wave_x = jnp.where(row == 1, NX // 2, row // 2).astype(jnp.float32)
    wave_y = jnp.where(col == 1, NY // 2, col // 2).astype(jnp.float32)
    damping = viscosity * (wave_x * wave_x + wave_y * wave_y)
    forced = (row == 0) & (col == 2 * forcing_wave)
    for a in range(2):
        for r in range(8):
            wave_t = (tm * 4 + r // 2).astype(jnp.float32)
            rate = frequency * wave_t if r % 2 == 0 else -frequency * wave_t
            term = rate * inputs[a][r ^ 1] + damping * inputs[a][r]
            if a == 0 and r == 0:
                force = jnp.where(tm == 0, -float(forcing_wave), 0.0).astype(jnp.float32)
                term = term - jnp.where(forced, force, 0.0)
            linear[a, r] = term

    for load in loads[2:]:
        load.wait()

    for a in range(2):
        settle(a_dst.at[a], recv_sem.at[0, a])
        value = time_transform(0, both(a_dst, a))
        for h in range(2):
            c1_src[a, h] = value[:, h * 128 : h * 128 + 128]
        gather_group(a)
        settle(c1_dst.at[a], recv_sem.at[1, a])
        for g in range(GROUP):
            for h in range(2):
                for t in range(2):
                    c2_src[a, lane_row(h, t, g), :] = c1_dst[a, g, h, t * OUTER : (t + 1) * OUTER, :]
        exchange_outer(2, a, c2_src, c2_dst)

    for a in range(2):
        settle(c2_dst.at[a], recv_sem.at[2, a])
        planes = []
        for t in range(2):
            columns = [
                jnp.concatenate([c2_dst[a, lane_row(h, t, g), :] for g in range(GROUP)], axis=0)
                for h in range(2)
            ]
            planes.append(jnp.concatenate(columns, axis=1))
        inverse = inverse_ref[...]
        right = halves(jnp.concatenate([inverse * planes[0], inverse * planes[1]] + planes, axis=1))
        for k, (along_x, along_y) in enumerate(((0, 6), (2, 4))):
            mixed = product((space_ref[along_x], space_ref[along_x + 1]), right)
            stacked = jnp.concatenate([mixed[:, q * 256 : q * 256 + 256] for q in range(4)], axis=0)
            grid = product(halves(stacked), (space_ref[along_y], space_ref[along_y + 1]))
            for q in range(4):
                fields[a, k, q] = grid[q * 256 : q * 256 + 256]
        points = []
        for t in range(2):
            total = fields[0, 0, t] * fields[a, 1, 2 + t] - fields[0, 1, t] * fields[a, 0, 2 + t]
            if a == 1:
                total = total + (
                    fields[1, 0, t] * fields[0, 1, 2 + t] - fields[1, 1, t] * fields[0, 0, 2 + t]
                )
            points.append(total)
        mixed = product((space_ref[8], space_ref[9]), halves(jnp.concatenate(points, axis=1)))
        stacked = jnp.concatenate([mixed[:, :256], mixed[:, 256:]], axis=0)
        modes = product(halves(stacked), (space_ref[10], space_ref[11]))
        for t in range(2):
            for g in range(GROUP):
                for h in range(2):
                    start = t * 256 + g * OUTER
                    r2_src[a, lane_row(h, t, g), :] = modes[
                        start : start + OUTER, h * 128 : h * 128 + 128
                    ]
        exchange_outer(3, a, r2_src, r2_dst)

    for a in range(2):
        settle(r2_dst.at[a], recv_sem.at[3, a])
        for g in range(GROUP):
            for h in range(2):
                for t in range(2):
                    r1_src[a, g, h, t * OUTER : (t + 1) * OUTER, :] = r2_dst[a, lane_row(h, t, g), :]
        scatter_group(a)
        settle(r1_dst.at[a], recv_sem.at[4, a])
        value = time_transform(2, both(r1_dst, a))
        for h in range(2):
            b_src[a, h] = value[:, h * 128 : h * 128 + 128]
        exchange_tm(5, a, b_src, b_dst)

    outputs = (residual_ref, jvp_ref)
    for a in range(2):
        settle(b_dst.at[a], recv_sem.at[5, a])
        for r in range(8):
            for h in range(2):
                lanes = slice(h * 128, h * 128 + 128)
                outputs[a][r, :, lanes] = linear[a, r, :, lanes] + b_dst[a, h, pl.ds(r, 64, stride=8), :]

    for a in range(2):
        settle(a_src.at[a, :, pl.ds(0, NT - 8)], send_sem.at[0, a])
        settle(c1_src.at[a, :, pl.ds(0, SPAN)], send_sem.at[1, a])
        settle(c2_src.at[a, pl.ds(0, 1024 - ROWS)], send_sem.at[2, a])
        settle(r2_src.at[a, pl.ds(0, 1024 - ROWS)], send_sem.at[3, a])
        settle(r1_src.at[a, 0], send_sem.at[4, a])
        settle(b_src.at[a, :, pl.ds(0, NT - 8)], send_sem.at[5, a])


PARTS = 2


def hand_over(residual_in, jvp_in, residual_ref, jvp_ref, sem):
    copies = []
    for a, (src, dst) in enumerate(((residual_in, residual_ref), (jvp_in, jvp_ref))):
        for k in range(PARTS):
            part = pl.ds(k * (8 // PARTS), 8 // PARTS)
            copies.append(pltpu.make_async_copy(src.at[part], dst.at[part], sem.at[a, k]))
    for copy in copies:
        copy.start()
    for copy in copies:
        copy.wait()


def solution(mesh):
    time, space, inverse = constants()

    def per_device(omega, delta):
        block = jax.ShapeDtypeStruct(omega.shape, jnp.float32)
        vmem, main = pl.BlockSpec(memory_space=pltpu.VMEM), pl.BlockSpec(memory_space=pltpu.HBM)
        held = pltpu.VMEM(omega.shape, jnp.float32)
        strips = pltpu.VMEM((2, 2, NT, 128), jnp.float32)
        pieces = pltpu.VMEM((2, GROUP, 2, SPAN, 128), jnp.float32)
        tiles = pltpu.VMEM((2, OUTER * ROWS, 128), jnp.float32)
        results = pl.pallas_call(
            kernel,
            out_shape=(held, held),
            in_specs=[main] * 5,
            out_specs=(vmem, vmem),
            scratch_shapes=[
                pltpu.VMEM(block.shape, jnp.float32),
                pltpu.VMEM(block.shape, jnp.float32),
                pltpu.VMEM(time.shape, jnp.bfloat16),
                pltpu.VMEM(space.shape, jnp.bfloat16),
                pltpu.VMEM(inverse.shape, jnp.float32),
                strips,
                strips,
                strips,
                pieces,
                tiles,
                tiles,
                pltpu.VMEM((2, 2, 4, NX, NY), jnp.float32),
                tiles,
                tiles,
                pieces,
                strips,
                strips,
                strips,
                pltpu.VMEM((2, 8, 64, NY), jnp.float32),
                pltpu.SemaphoreType.DMA((5,)),
                pltpu.SemaphoreType.DMA((6, 2)),
                pltpu.SemaphoreType.DMA((6, 2)),
                pltpu.SemaphoreType.REGULAR,
            ],
            compiler_params=pltpu.CompilerParams(
                collective_id=0, has_side_effects=True, vmem_limit_bytes=58 * 1024 * 1024
            ),
        )(omega, delta, time, space, inverse)
        return pl.pallas_call(
            hand_over,
            out_shape=(block, block),
            in_specs=[vmem] * 2,
            out_specs=(main, main),
            scratch_shapes=[pltpu.SemaphoreType.DMA((2, PARTS))],
        )(*[pltpu.with_memory_space_constraint(result, pltpu.VMEM) for result in results])

    specs = (P("tm", "space", None), P("tm", "space", None))
    return jax.shard_map(per_device, mesh=mesh, in_specs=specs, out_specs=specs, check_vma=False)
```

```python
import functools

import jax
import jax.numpy as jnp
import ml_dtypes
import numpy as np
from jax import lax
from jax.experimental import pallas as pl
from jax.experimental.pallas import tpu as pltpu
from jax.sharding import PartitionSpec as P

MESH = pl.DeviceIdType.MESH
viscosity = 0.025
frequency = 0.3
forcing_wave = 4

NT, NX, NY = 512, 256, 256
GROUP = 2
OUTER = 256 // GROUP
ROWS = 4 * GROUP
SPAN = NT // GROUP


def wavenumbers(n):
    indices = np.arange(n)
    return np.where(indices == 1, n // 2, indices // 2)


def basis_matrix(n):
    points, indices, wave = np.arange(n), np.arange(n), wavenumbers(n)
    angles = (points[:, None] * wave[None, :] % n) * (2.0 * np.pi / n)
    is_sine = (indices % 2 == 1) & (indices != 1)
    return np.where(is_sine[None, :], np.sin(angles), np.cos(angles))


def forward_matrix(n):
    weights = np.where(np.arange(n) < 2, 1.0 / n, 2.0 / n)
    return basis_matrix(n).T * weights[:, None]


def derivative_matrix(n):
    wave = wavenumbers(n)
    out = np.zeros((n, n))
    for j in range(2, n):
        if j % 2 == 0:
            out[j, j + 1] = wave[j]
        else:
            out[j, j - 1] = -wave[j]
    return out


def split_constant(matrix):
    high = matrix.astype(np.float32).astype(ml_dtypes.bfloat16)
    low = (matrix - high.astype(np.float64)).astype(np.float32).astype(ml_dtypes.bfloat16)
    return [high, low]


def x_order():
    core, x_hi, tm = np.meshgrid(np.arange(2), np.arange(2), np.arange(64), indexing="ij")
    return (128 * x_hi + 64 * core + tm).reshape(-1)


def constants():
    order = x_order()
    synth_t, forward_t = basis_matrix(NT), forward_matrix(NT)
    synth_x, synth_y = basis_matrix(NX), basis_matrix(NY)
    slope_x = (synth_x @ derivative_matrix(NX))[:, order]
    slope_y = synth_y @ derivative_matrix(NY)
    time = np.stack(split_constant(synth_t) + split_constant(forward_t))
    space = np.stack(
        split_constant(synth_x[:, order])
        + split_constant(slope_x)
        + split_constant(synth_y.T)
        + split_constant(slope_y.T)
        + split_constant(forward_matrix(NX)[order])
        + split_constant(forward_matrix(NY).T)
    )
    wave_x, wave_y = wavenumbers(NX)[order], wavenumbers(NY)
    square = (wave_x[:, None] ** 2 + wave_y[None, :] ** 2).astype(np.float64)
    inverse = np.where(square > 0, 1.0 / np.maximum(square, 1.0), 0.0).astype(np.float32)
    return time, space, inverse


def halves(value):
    high = value.astype(jnp.bfloat16)
    return high, (value - high.astype(jnp.float32)).astype(jnp.bfloat16)


def product(left, right):
    dot = functools.partial(jnp.dot, preferred_element_type=jnp.float32)
    return dot(left[0], right[0]) + (dot(left[1], right[0]) + dot(left[0], right[1]))


def both(ref, *index):
    return jnp.concatenate([ref[(*index, h)] for h in range(2)], axis=1)


def kernel(
    omega_hbm,
    delta_hbm,
    time_hbm,
    space_hbm,
    inverse_hbm,
    residual_ref,
    jvp_ref,
    omega_ref,
    delta_ref,
    time_ref,
    space_ref,
    inverse_ref,
    a_src,
    a_dst,
    c1_src,
    c1_dst,
    c2_src,
    c2_dst,
    fields,
    r2_src,
    r2_dst,
    r1_src,
    r1_dst,
    b_src,
    b_dst,
    linear,
    const_sem,
    send_sem,
    recv_sem,
    plane_sem,
):
    tm, space = lax.axis_index("tm"), lax.axis_index("space")
    z, y, x_lo, x_hi, core = tm // 8, (tm // 2) % 4, tm % 2, space // 2, space % 2
    outer = x_hi * 64 + tm
    inputs = (omega_ref, delta_ref)

    loads = [
        pltpu.make_async_copy(src, dst, const_sem.at[k])
        for k, (src, dst) in enumerate(
            (
                (omega_hbm, omega_ref),
                (delta_hbm, delta_ref),
                (time_hbm, time_ref),
                (space_hbm, space_ref),
                (inverse_hbm, inverse_ref),
            )
        )
    ]

    barrier = pltpu.get_barrier_semaphore()
    column = [(((z + dz) % 8) * 8 + y * 2 + x_lo, space) for dz in (4, 3, 5, 2, 6, 1, 7)]
    greeted = []
    for dy in (2, 1, 3, 0):
        for dx in (2, 1, 3, 0):
            if dy or dx:
                x = (x_hi * 2 + x_lo + dx) % 4
                greeted.append((z * 8 + ((y + dy) % 4) * 2 + x % 2, (x // 2) * 2 + core))
    greeted = greeted[:1] + column[:3] + greeted[1:] + column[3:] + [(tm, x_hi * 2 + (1 - core))]
    for device in greeted:
        pl.semaphore_signal(barrier, inc=1, device_id=device, device_id_type=MESH)
    for load in loads:
        load.start()

    def tm_partner(step):
        dz, place = 3 * step, step // 8
        return ((z + dz) % 8) * 8 + ((y + place // 2) % 4) * 2 + (x_lo + place) % 2

    def by_plane(step):
        plane, place = step // 8, step % 8
        return plane * 8 + ((y + place // 2) % 4) * 2 + (x_lo + place) % 2

    def outer_partner(step):
        dz, place = 3 * step, step // 8
        x = (x_hi * 2 + x_lo + place) % 4
        return ((z + dz) % 8) * 8 + ((y + place // 4) % 4) * 2 + x % 2, x // 2

    def settle(buffer, sem):
        pltpu.make_async_copy(buffer, buffer, sem).wait()

    def rows8(index):
        return pl.ds(pl.multiple_of(index * 8, 8), 8)

    def exchange_tm(stage, a, src, dst, first=0, last=64, order=None):
        send, recv = send_sem.at[stage, a], recv_sem.at[stage, a]
        if first == 0:
            pltpu.make_async_copy(src.at[a, :, rows8(tm)], dst.at[a, :, rows8(tm)], recv).start()

        def body(step, carry):
            partner = (order or tm_partner)(step)

            def send_one():
                pltpu.make_async_remote_copy(
                    src_ref=src.at[a, :, rows8(partner)],
                    dst_ref=dst.at[a, :, rows8(tm)],
                    send_sem=send,
                    recv_sem=recv,
                    device_id=(partner, space),
                    device_id_type=MESH,
                ).start()

            if order is None:
                send_one()
            else:
                pl.when(partner != tm)(send_one)
            return carry

        lax.fori_loop(first if order else max(first, 1), last, body, 0)

    def message(index):
        return pl.ds(pl.multiple_of(index * ROWS, ROWS), ROWS)

    def exchange_outer(stage, a, src, dst):
        send, recv = send_sem.at[stage, a], recv_sem.at[stage, a]
        pltpu.make_async_copy(src.at[a, message(outer)], dst.at[a, message(outer)], recv).start()

        def body(step, carry):
            partner, partner_hi = outer_partner(step)
            pltpu.make_async_remote_copy(
                src_ref=src.at[a, message(partner_hi * 64 + partner)],
                dst_ref=dst.at[a, message(outer)],
                send_sem=send,
                recv_sem=recv,
                device_id=(partner, partner_hi * 2 + core),
                device_id_type=MESH,
            ).start()
            return carry

        lax.fori_loop(1, OUTER, body, 0)

    def span(index):
        return pl.ds(pl.multiple_of(index * SPAN, SPAN), SPAN)

    sibling = (tm, x_hi * 2 + (1 - core))

    def gather_group(a):
        send, recv = send_sem.at[1, a], recv_sem.at[1, a]
        pltpu.make_async_copy(c1_src.at[a, :, span(core)], c1_dst.at[a, core], recv).start()
        pltpu.make_async_remote_copy(
            src_ref=c1_src.at[a, :, span(1 - core)],
            dst_ref=c1_dst.at[a, core],
            send_sem=send,
            recv_sem=recv,
            device_id=sibling,
            device_id_type=MESH,
        ).start()

    def scatter_group(a):
        send, recv = send_sem.at[4, a], recv_sem.at[4, a]
        pltpu.make_async_copy(r1_src.at[a, core], r1_dst.at[a, :, span(core)], recv).start()
        pltpu.make_async_remote_copy(
            src_ref=r1_src.at[a, 1 - core],
            dst_ref=r1_dst.at[a, :, span(core)],
            send_sem=send,
            recv_sem=recv,
            device_id=sibling,
            device_id_type=MESH,
        ).start()

    def time_transform(which, value):
        matrix = (time_ref[which], time_ref[which + 1])
        return product(matrix, halves(value))

    def lane_row(half, point, member):
        return pl.ds((half * 2 + point) * GROUP + member, OUTER, stride=ROWS)

    for a in range(2):
        loads[a].wait()
        for r in range(8):
            for h in range(2):
                a_src[a, h, pl.ds(r, 64, stride=8), :] = inputs[a][r, :, h * 128 : h * 128 + 128]
    pl.semaphore_wait(barrier, len(greeted))
    for device in column:
        pl.semaphore_signal(plane_sem, inc=1, device_id=device, device_id_type=MESH)
    for a in range(2):
        exchange_tm(0, a, a_src, a_dst, 0, 8)
    pl.semaphore_wait(plane_sem, len(column))
    for a in range(2):
        exchange_tm(0, a, a_src, a_dst, 8, 64)

    row = lax.broadcasted_iota(jnp.int32, (64, NY), 0) + space * 64
    col = lax.broadcasted_iota(jnp.int32, (64, NY), 1)
    wave_x = jnp.where(row == 1, NX // 2, row // 2).astype(jnp.float32)
    wave_y = jnp.where(col == 1, NY // 2, col // 2).astype(jnp.float32)
    damping = viscosity * (wave_x * wave_x + wave_y * wave_y)
    forced = (row == 0) & (col == 2 * forcing_wave)
    for a in range(2):
        for r in range(8):
            wave_t = (tm * 4 + r // 2).astype(jnp.float32)
            rate = frequency * wave_t if r % 2 == 0 else -frequency * wave_t
            term = rate * inputs[a][r ^ 1] + damping * inputs[a][r]
            if a == 0 and r == 0:
                force = jnp.where(tm == 0, -float(forcing_wave), 0.0).astype(jnp.float32)
                term = term - jnp.where(forced, force, 0.0)
            linear[a, r] = term

    for load in loads[2:]:
        load.wait()

    for a in range(2):
        settle(a_dst.at[a], recv_sem.at[0, a])
        value = time_transform(0, both(a_dst, a))
        for h in range(2):
            c1_src[a, h] = value[:, h * 128 : h * 128 + 128]
        gather_group(a)
        settle(c1_dst.at[a], recv_sem.at[1, a])
        for g in range(GROUP):
            for h in range(2):
                for t in range(2):
                    c2_src[a, lane_row(h, t, g), :] = c1_dst[a, g, h, t * OUTER : (t + 1) * OUTER, :]
        exchange_outer(2, a, c2_src, c2_dst)

    for a in range(2):
        settle(c2_dst.at[a], recv_sem.at[2, a])
        planes = []
        for t in range(2):
            columns = [
                jnp.concatenate([c2_dst[a, lane_row(h, t, g), :] for g in range(GROUP)], axis=0)
                for h in range(2)
            ]
            planes.append(jnp.concatenate(columns, axis=1))
        inverse = inverse_ref[...]
        right = halves(jnp.concatenate([inverse * planes[0], inverse * planes[1]] + planes, axis=1))
        for k, (along_x, along_y) in enumerate(((0, 6), (2, 4))):
            mixed = product((space_ref[along_x], space_ref[along_x + 1]), right)
            stacked = jnp.concatenate([mixed[:, q * 256 : q * 256 + 256] for q in range(4)], axis=0)
            grid = product(halves(stacked), (space_ref[along_y], space_ref[along_y + 1]))
            for q in range(4):
                fields[a, k, q] = grid[q * 256 : q * 256 + 256]
        points = []
        for t in range(2):
            total = fields[0, 0, t] * fields[a, 1, 2 + t] - fields[0, 1, t] * fields[a, 0, 2 + t]
            if a == 1:
                total = total + (
                    fields[1, 0, t] * fields[0, 1, 2 + t] - fields[1, 1, t] * fields[0, 0, 2 + t]
                )
            points.append(total)
        mixed = product((space_ref[8], space_ref[9]), halves(jnp.concatenate(points, axis=1)))
        stacked = jnp.concatenate([mixed[:, :256], mixed[:, 256:]], axis=0)
        modes = product(halves(stacked), (space_ref[10], space_ref[11]))
        for t in range(2):
            for g in range(GROUP):
                for h in range(2):
                    start = t * 256 + g * OUTER
                    r2_src[a, lane_row(h, t, g), :] = modes[
                        start : start + OUTER, h * 128 : h * 128 + 128
                    ]
        exchange_outer(3, a, r2_src, r2_dst)

    for a in range(2):
        settle(r2_dst.at[a], recv_sem.at[3, a])
        for g in range(GROUP):
            for h in range(2):
                for t in range(2):
                    r1_src[a, g, h, t * OUTER : (t + 1) * OUTER, :] = r2_dst[a, lane_row(h, t, g), :]
        scatter_group(a)
        settle(r1_dst.at[a], recv_sem.at[4, a])
        value = time_transform(2, both(r1_dst, a))
        for h in range(2):
            b_src[a, h] = value[:, h * 128 : h * 128 + 128]
        exchange_tm(5, a, b_src, b_dst, order=by_plane)

    outputs = (residual_ref, jvp_ref)
    for a in range(2):
        settle(b_dst.at[a], recv_sem.at[5, a])
        for r in range(8):
            for h in range(2):
                lanes = slice(h * 128, h * 128 + 128)
                outputs[a][r, :, lanes] = linear[a, r, :, lanes] + b_dst[a, h, pl.ds(r, 64, stride=8), :]

    for a in range(2):
        settle(a_src.at[a, :, pl.ds(0, NT - 8)], send_sem.at[0, a])
        settle(c1_src.at[a, :, pl.ds(0, SPAN)], send_sem.at[1, a])
        settle(c2_src.at[a, pl.ds(0, 1024 - ROWS)], send_sem.at[2, a])
        settle(r2_src.at[a, pl.ds(0, 1024 - ROWS)], send_sem.at[3, a])
        settle(r1_src.at[a, 0], send_sem.at[4, a])
        settle(b_src.at[a, :, pl.ds(0, NT - 8)], send_sem.at[5, a])


PARTS = 2


def hand_over(residual_in, jvp_in, residual_ref, jvp_ref, sem):
    copies = []
    for a, (src, dst) in enumerate(((residual_in, residual_ref), (jvp_in, jvp_ref))):
        for k in range(PARTS):
            part = pl.ds(k * (8 // PARTS), 8 // PARTS)
            copies.append(pltpu.make_async_copy(src.at[part], dst.at[part], sem.at[a, k]))
    for copy in copies:
        copy.start()
    for copy in copies:
        copy.wait()


def solution(mesh):
    time, space, inverse = constants()

    def per_device(omega, delta):
        block = jax.ShapeDtypeStruct(omega.shape, jnp.float32)
        vmem, main = pl.BlockSpec(memory_space=pltpu.VMEM), pl.BlockSpec(memory_space=pltpu.HBM)
        held = pltpu.VMEM(omega.shape, jnp.float32)
        strips = pltpu.VMEM((2, 2, NT, 128), jnp.float32)
        pieces = pltpu.VMEM((2, GROUP, 2, SPAN, 128), jnp.float32)
        tiles = pltpu.VMEM((2, OUTER * ROWS, 128), jnp.float32)
        results = pl.pallas_call(
            kernel,
            out_shape=(held, held),
            in_specs=[main] * 5,
            out_specs=(vmem, vmem),
            scratch_shapes=[
                pltpu.VMEM(block.shape, jnp.float32),
                pltpu.VMEM(block.shape, jnp.float32),
                pltpu.VMEM(time.shape, jnp.bfloat16),
                pltpu.VMEM(space.shape, jnp.bfloat16),
                pltpu.VMEM(inverse.shape, jnp.float32),
                strips,
                strips,
                strips,
                pieces,
                tiles,
                tiles,
                pltpu.VMEM((2, 2, 4, NX, NY), jnp.float32),
                tiles,
                tiles,
                pieces,
                strips,
                strips,
                strips,
                pltpu.VMEM((2, 8, 64, NY), jnp.float32),
                pltpu.SemaphoreType.DMA((5,)),
                pltpu.SemaphoreType.DMA((6, 2)),
                pltpu.SemaphoreType.DMA((6, 2)),
                pltpu.SemaphoreType.REGULAR,
            ],
            compiler_params=pltpu.CompilerParams(
                collective_id=0, has_side_effects=True, vmem_limit_bytes=58 * 1024 * 1024
            ),
        )(omega, delta, time, space, inverse)
        return pl.pallas_call(
            hand_over,
            out_shape=(block, block),
            in_specs=[vmem] * 2,
            out_specs=(main, main),
            scratch_shapes=[pltpu.SemaphoreType.DMA((2, PARTS))],
        )(*[pltpu.with_memory_space_constraint(result, pltpu.VMEM) for result in results])

    specs = (P("tm", "space", None), P("tm", "space", None))
    return jax.shard_map(per_device, mesh=mesh, in_specs=specs, out_specs=specs, check_vma=False)
```
